32 devices in a mesh: blk: 16 (over z, x, core), uly: 2 (over y).
Axes of the slice: x: 2, y: 2, z: 4, core: 2. Of those that a mesh axis runs over, the one named last changes fastest.
Arguments:
- tokens: bfloat16 [8192, 1024], P(('blk', 'uly')), may hold values from -32 to 32
- w_qkv: bfloat16 [1024, 3072], replicated, may hold values from -0.1875 to 0.1875
- w_out: bfloat16 [1024, 1024], replicated, may hold values from -0.1875 to 0.1875
- band: int32 [64], P('blk'), may hold values from 1 to 8, as said below
- global_ids: int32 [4], replicated, may hold values from 0 to 63, as said below
Outputs:
- mixed: bfloat16 [8192, 1024], P(('blk', 'uly'))
The draws below stay inside these ranges and needn't reach their ends.
Inputs may be any that keep to these rules, and one draw needn't show every extreme that they name: `band`: every value from 1 to 8 may occur; both ends occur. `global_ids`: distinct block ids; the first and the last block are among them.
All inputs are finite; a program needn't handle non-finite values.
Results may differ from the reference program's by a relative error of at most 0.007.
The reference program's roundings to bfloat16 on the way (of `qkv` and `attended`) count: a program that leaves them out, or rounds other values in their place, can miss the bound.
Values may be sent and summed in bfloat16 or wider, within the bound.
A program may use at most 64 MiB of HBM per device.

```python
import jax
import jax.numpy as jnp
from jax import lax

D = 1024
H = 8
HD = 128
NGLOBAL = 4
TOKENS = 8192
QBLOCKS = 64
MAXBAND = 8


def draw_tokens(key, part):
    key = jax.random.fold_in(key, 11)
    values = jax.random.truncated_normal(key, -3.0, 3.0, (TOKENS, D), jnp.float32)
    return values.astype(jnp.bfloat16)


def draw_band(key, part):
    key = jax.random.fold_in(key, 21)
    widths = jax.random.randint(key, (QBLOCKS,), 1, MAXBAND + 1)
    where_top = jax.random.randint(jax.random.fold_in(key, 1), (), 0, QBLOCKS)
    widths = widths.at[where_top].set(MAXBAND)
    widths = widths.at[(where_top + 1) % QBLOCKS].set(1)
    return widths.astype(jnp.int32)


def draw_global_ids(key, part):
    key = jax.random.fold_in(key, 31)
    middle = jax.random.permutation(key, QBLOCKS - 2)[:NGLOBAL - 2] + 1
    first = jnp.zeros((1,), jnp.int32)
    last = jnp.full((1,), QBLOCKS - 1, jnp.int32)
    return jnp.concatenate([first, middle.astype(jnp.int32), last]).astype(jnp.int32)


def noise(stream_key, extent, width, most, kind=jnp.bfloat16):
    drawn = jax.random.normal(stream_key, extent, jnp.float32) * width
    return jnp.minimum(jnp.maximum(drawn, -most), most).astype(kind)


def setup_inputs(seed: int = 0) -> dict:
    streams_of = jax.random.split(jax.random.key(seed), 6)
    tokens = draw_tokens(jax.random.fold_in(streams_of[5], 71), 0)
    w_qkv = noise(streams_of[1], (D, 3 * D), D ** -0.5, 0.1875)
    w_out = noise(streams_of[2], (D, D), D ** -0.5, 0.1875)
    band = draw_band(jax.random.fold_in(streams_of[5], 71), 0)
    global_ids = draw_global_ids(jax.random.fold_in(streams_of[5], 71), 0)
    return dict(tokens=tokens, w_qkv=w_qkv, w_out=w_out, band=band, global_ids=global_ids)


def reference(tokens, w_qkv, w_out, band, global_ids):
    qkv = jnp.dot(tokens, w_qkv, preferred_element_type=jnp.float32).astype(jnp.bfloat16)
    qkv = qkv.reshape(TOKENS, 3, H, HD)
    queries = qkv[:, 0]
    keys = qkv[:, 1]
    values = qkv[:, 2]
    padding = MAXBAND * 128
    keys_padded = jnp.pad(keys, ((padding, padding), (0, 0), (0, 0)))
    values_padded = jnp.pad(values, ((padding, padding), (0, 0), (0, 0)))
    global_rows = (global_ids[:, None] * 128 + jnp.arange(128, dtype=jnp.int32)[None, :]).reshape(-1)
    global_keys = keys[global_rows]
    global_values = values[global_rows]
    window = (2 * MAXBAND + 1) * 128
    score_scale = 1.0 / (HD ** 0.5)

    def attend_block(q_block):
        start = (q_block * 128).astype(jnp.int32)
        q_rows = lax.dynamic_slice_in_dim(queries, start, 128, 0)
        key_window = lax.dynamic_slice_in_dim(keys_padded, start, window, 0)
        value_window = lax.dynamic_slice_in_dim(values_padded, start, window, 0)
        all_keys = jnp.concatenate([key_window, global_keys], 0).astype(jnp.float32)
        all_values = jnp.concatenate([value_window, global_values], 0)
        scores = jnp.einsum("qhd,khd->hqk", q_rows.astype(jnp.float32), all_keys) * score_scale
        width_here = band[q_block]
        key_blocks = q_block - MAXBAND + jnp.arange(window, dtype=jnp.int32) // 128
        in_window = (key_blocks >= 0) & (key_blocks < QBLOCKS) & (jnp.abs(key_blocks - q_block) <= width_here)
        in_global = jnp.repeat(jnp.abs(global_ids - q_block) > width_here, 128)
        allowed = jnp.concatenate([in_window, in_global])
        scores = jnp.where(allowed[None, None, :], scores, -jnp.inf)
        highest = jnp.max(scores, axis=-1, keepdims=True)
        weights = jnp.exp(scores - highest)
        totals = jnp.sum(weights, axis=-1)
        rounded = weights.astype(jnp.bfloat16).astype(jnp.float32)
        result = jnp.einsum("hqk,khd->qhd", rounded, all_values.astype(jnp.float32))
        result = result / jnp.transpose(totals)[:, :, None]
        return result.astype(jnp.bfloat16)

    attended = lax.map(attend_block, jnp.arange(QBLOCKS, dtype=jnp.int32)).reshape(TOKENS, D)
    return jnp.dot(attended, w_out, preferred_element_type=jnp.float32).astype(jnp.bfloat16)
```

```python
import functools
import math

import jax
import jax.numpy as jnp
from jax import lax
from jax.experimental import pallas as pl
from jax.experimental.pallas import tpu as pltpu
from jax.sharding import PartitionSpec as P

H = 8
HD = 128
BLOCK = 128
NGLOBAL = 4
REACH = 2
SLOTS = 2 * REACH + 1
VMEM_LIMIT = 56 * 1024 * 1024
EXP2_SCALE = math.log2(math.e) / HD**0.5
MASKED = -1e30


def gather_kernel(
    nb, nu, ids_ref, tok_ref, w_ref, q_ref, win_ref, glob_ref,
    qkv_ref, own_ref, pre_ref, suf_ref, up_ref, down_ref,
    a2a_s, a2a_r, x_s, x_r, c_s, c_r, f_s, f_r, z_s, z_r,
    up_s, up_r, dn_s, dn_r, gx_s, gx_r, gc_s, gc_r, gf_s, gf_r,
):
    tok = tok_ref.shape[0]
    hd = H // nu
    ctx = tok * nu
    bd = ctx // BLOCK
    nz = nb // 4
    half = NGLOBAL // 2
    nj = 2 * hd
    b = lax.axis_index("blk")
    u = lax.axis_index("uly")
    r = b % 4
    z = b // 4
    low = r < 2
    inner = (r == 1) | (r == 2)
    has_up = z < nz - 1
    has_dn = z > 0
    px = jnp.where(low, b + 2, b - 2)
    pc = jnp.where(r % 2 == 0, b + 1, b - 1)

    barrier = pltpu.get_barrier_semaphore()

    def greet(blk, uly):
        pl.semaphore_signal(
            barrier, inc=1, device_id=(blk, uly), device_id_type=pl.DeviceIdType.MESH
        )

    for d in range(1, nu):
        greet(b, (u + d) % nu)
    greet(px, u)
    greet(pc, u)
    pl.when(has_up)(lambda: greet(b + 4, u))
    pl.when(has_dn)(lambda: greet(b - 4, u))
    pl.semaphore_wait(
        barrier, nu + 1 + jnp.where(has_up, 1, 0) + jnp.where(has_dn, 1, 0)
    )

    def rdma(src, dst, s, rr, blk, uly):
        return pltpu.make_async_remote_copy(
            src_ref=src, dst_ref=dst, send_sem=s, recv_sem=rr,
            device_id=(blk, uly), device_id_type=pl.DeviceIdType.MESH,
        )

    def slot(j, s):
        return win_ref.at[j, pl.ds(pl.multiple_of(s * ctx, ctx), ctx)]

    def clear(s):
        win_ref[:, pl.ds(s * ctx, ctx), :] = jnp.zeros((nj, ctx, HD), jnp.bfloat16)

    pl.when(b < 2)(lambda: clear(0))
    pl.when(b < 1)(lambda: clear(1))
    pl.when(b > nb - 2)(lambda: clear(3))
    pl.when(b > nb - 3)(lambda: clear(4))

    def a2a(d, j, part, h):
        to = (u + d) % nu
        rows = pl.ds(pl.multiple_of(u * tok, tok), tok)
        if part == 0:
            dst = q_ref.at[h, rows]
        else:
            dst = win_ref.at[
                (part - 1) * hd + h, pl.ds(pl.multiple_of(2 * ctx + u * tok, tok), tok)
            ]
        return rdma(
            qkv_ref.at[part * H + to * hd + h], dst,
            a2a_s.at[d - 1, j], a2a_r.at[d - 1, j], b, to,
        )

    def chunks(part):
        return [(j, j - {1: 0, 2: hd, 0: 2 * hd}[part])
                for j in range({1: 0, 2: hd, 0: 2 * hd}[part], {1: hd, 2: 2 * hd, 0: 3 * hd}[part])]

    for part in (1, 2, 0):
        for p in range(H // 2):
            col = part * H * HD + p * 2 * HD
            res = jnp.dot(
                tok_ref[...], w_ref[:, col:col + 2 * HD], preferred_element_type=jnp.float32
            ).astype(jnp.bfloat16)
            qkv_ref[part * H + 2 * p] = res[:, :HD]
            qkv_ref[part * H + 2 * p + 1] = res[:, HD:]
        for j, h in chunks(part):
            for d in range(1, nu):
                a2a(d, j, part, h).start()
        for j, h in chunks(part):
            mine = qkv_ref[part * H + u * hd + h]
            if part == 0:
                q_ref[h, pl.ds(pl.multiple_of(u * tok, tok), tok)] = mine
            else:
                win_ref[j, pl.ds(pl.multiple_of(2 * ctx + u * tok, tok), tok)] = mine

    s_x = jnp.where(low, 0, 4)
    s_c = jnp.where(r % 2 == 0, 1, 3)
    in_x = 4 - s_x
    f_src = jnp.where((r == 0) | (r == 2), 4, 0)
    f_dst = jnp.where((r == 0) | (r == 2), 3, 1)

    def x_copy(j):
        return rdma(slot(j, 2), slot(j, s_x), x_s.at[j], x_r.at[j], px, u)

    def c_copy(j):
        return rdma(slot(j, 2), slot(j, s_c), c_s.at[j], c_r.at[j], pc, u)

    def f_copy(j):
        return rdma(slot(j, f_src), slot(j, f_dst), f_s.at[j], f_r.at[j], pc, u)

    z_to = jnp.where(low, b + 4, b - 4)
    z_sends = (low & has_up) | (~low & has_dn)
    z_gets = (low & has_dn) | (~low & has_up)
    f_sends = (r == 0) | (r == 3) | z_gets
    f_gets = inner | z_gets

    def z_copy(j):
        return rdma(slot(j, in_x), slot(j, s_x), z_s.at[j], z_r.at[j], z_to, u)

    def stage_a(j):
        part = 1 + j // hd
        for d in range(1, nu):
            a2a(d, j, part, j % hd).wait_recv()
        x_copy(j).start()
        c_copy(j).start()

    def stage_b(j):
        x_copy(j).wait_recv()
        pl.when((r == 0) | (r == 3))(lambda: f_copy(j).start())
        pl.when(z_sends)(lambda: z_copy(j).start())

    def stage_c(j):
        @pl.when(z_gets)
        def _():
            z_copy(j).wait_recv()
            pl.when(inner)(lambda: f_copy(j).start())
        c_copy(j).wait_recv()

        @pl.when(inner)
        def _():
            f_copy(j).wait_recv()
            first = jnp.where(r == 1, 1, 0)
            for g in range(half):
                gid = jnp.where(r == 1, ids_ref[g], ids_ref[half + g]) - 4 * z * bd

                def add(i, acc):
                    blk = win_ref[j, pl.ds(pl.multiple_of((first * bd + i) * BLOCK, BLOCK), BLOCK)]
                    take = jnp.where(gid == i, 1.0, 0.0).astype(jnp.float32)
                    return acc + blk.astype(jnp.float32) * take

                acc = lax.fori_loop(0, 4 * bd, add, jnp.zeros((BLOCK, HD), jnp.float32))
                own_ref[j, g * BLOCK:(g + 1) * BLOCK] = acc.astype(jnp.bfloat16)

    def up_copy(j):
        return rdma(up_ref.at[j], pre_ref.at[j], up_s.at[j], up_r.at[j], b + 4, u)

    def dn_copy(j):
        return rdma(down_ref.at[j], suf_ref.at[j], dn_s.at[j], dn_r.at[j], b - 4, u)

    def wait_in(kind, other, sem_s, sem_r, j):
        rdma(kind.at[j], kind.at[j], sem_s.at[j], sem_r.at[j], other, u).wait_recv()

    def stage_up(j):
        @pl.when(inner)
        def _():
            @pl.when(has_dn)
            def _():
                wait_in(pre_ref, b - 4, up_s, up_r, j)

            @pl.when(~has_dn)
            def _():
                pre_ref[j] = jnp.zeros((half * BLOCK, HD), jnp.bfloat16)

            @pl.when(has_up)
            def _():
                up_ref[j] = pre_ref[j] + own_ref[j]
                up_copy(j).start()

    a_half = pl.ds(0, half * BLOCK)
    b_half = pl.ds(half * BLOCK, half * BLOCK)
    mine_half = pl.ds(pl.multiple_of(jnp.where(r == 1, 0, half * BLOCK), BLOCK), half * BLOCK)
    fwd_half = pl.ds(pl.multiple_of(jnp.where(r == 0, half * BLOCK, 0), BLOCK), half * BLOCK)

    def gx_copy(j):
        return rdma(glob_ref.at[j, mine_half], glob_ref.at[j, mine_half],
                    gx_s.at[j], gx_r.at[j], px, u)

    def gc_copy(j):
        return rdma(glob_ref.at[j, mine_half], glob_ref.at[j, mine_half],
                    gc_s.at[j], gc_r.at[j], pc, u)

    def gf_copy(j):
        return rdma(glob_ref.at[j, fwd_half], glob_ref.at[j, fwd_half],
                    gf_s.at[j], gf_r.at[j], pc, u)

    def stage_down(j):
        @pl.when(inner)
        def _():
            @pl.when(has_up)
            def _():
                wait_in(suf_ref, b + 4, dn_s, dn_r, j)

            @pl.when(~has_up)
            def _():
                suf_ref[j] = jnp.zeros((half * BLOCK, HD), jnp.bfloat16)

            total = suf_ref[j] + own_ref[j]

            @pl.when(has_dn)
            def _():
                down_ref[j] = total
                dn_copy(j).start()

            glob_ref[j, mine_half] = total + pre_ref[j]
            gx_copy(j).start()
            gc_copy(j).start()

    def stage_out(j):
        @pl.when(~inner)
        def _():
            gx_copy(j).wait_recv()
            gf_copy(j).start()

    stages = [(0, stage_a), (1, stage_b), (2, stage_c), (3, stage_up), (5, stage_down), (6, stage_out)]
    for t in range(nj + 6):
        for lag, stage in stages:
            if 0 <= t - lag < nj:
                stage(t - lag)

    for part in (1, 2, 0):
        for j, h in chunks(part):
            for d in range(1, nu):
                a2a(d, j, part, h).wait_send()
                if part == 0:
                    a2a(d, j, part, h).wait_recv()
    for j in range(nj):
        x_copy(j).wait_send()
        c_copy(j).wait_send()
        pl.when(f_sends)(lambda: f_copy(j).wait_send())
        pl.when(z_sends)(lambda: z_copy(j).wait_send())
        pl.when(f_gets & ~inner)(lambda: f_copy(j).wait_recv())

        @pl.when(inner)
        def _():
            pl.when(has_up)(lambda: up_copy(j).wait_send())
            pl.when(has_dn)(lambda: dn_copy(j).wait_send())
            gx_copy(j).wait_send()
            gc_copy(j).wait_send()
            gf_copy(j).wait_recv()

        @pl.when(~inner)
        def _():
            gc_copy(j).wait_recv()
            gf_copy(j).wait_send()


def gather(nb, nu, global_ids, tokens, w_qkv):
    tok = tokens.shape[0]
    hd = H // nu
    ctx = tok * nu
    nj = 2 * hd
    part = pltpu.VMEM((nj, NGLOBAL // 2 * BLOCK, HD), jnp.bfloat16)
    dma = pltpu.SemaphoreType.DMA
    vmem = pl.BlockSpec(memory_space=pltpu.VMEM)
    return pl.pallas_call(
        functools.partial(gather_kernel, nb, nu),
        out_shape=[
            jax.ShapeDtypeStruct((hd, ctx, HD), jnp.bfloat16),
            jax.ShapeDtypeStruct((nj, SLOTS * ctx, HD), jnp.bfloat16),
            jax.ShapeDtypeStruct((nj, NGLOBAL * BLOCK, HD), jnp.bfloat16),
        ],
        in_specs=[pl.BlockSpec(memory_space=pltpu.SMEM), vmem, vmem],
        out_specs=[vmem, vmem, vmem],
        scratch_shapes=[
            pltpu.VMEM((3 * H, tok, HD), jnp.bfloat16), part, part, part, part, part,
            dma((nu - 1, 3 * hd)), dma((nu - 1, 3 * hd)),
        ] + [dma((nj,))] * 18,
        compiler_params=pltpu.CompilerParams(
            collective_id=0, has_side_effects=True, vmem_limit_bytes=VMEM_LIMIT
        ),
    )(global_ids, tokens, w_qkv)


def attend_kernel(nb, nu, band_ref, ids_ref, q_ref, win_ref, glob_ref, out_ref):
    hd = H // nu
    ctx = q_ref.shape[1]
    bd = ctx // BLOCK
    reach = REACH * bd
    window = (2 * reach + 1) * BLOCK
    b = lax.axis_index("blk")
    nt = (((1,), (1,)), ((), ()))

    @pl.loop(0, bd)
    def _(lb):
        q_block = b * bd + lb
        width = band_ref[lb]
        key = q_block - reach + lax.broadcasted_iota(jnp.int32, (1, window), 1) // BLOCK
        seen = (jnp.abs(key - q_block) <= width) & (key >= 0) & (key < nb * bd)
        bias_w = jnp.where(seen, 0.0, MASKED)
        lane = lax.broadcasted_iota(jnp.int32, (1, NGLOBAL * BLOCK), 1) // BLOCK
        gid = jnp.zeros_like(lane)
        for g in range(NGLOBAL):
            gid = jnp.where(lane == g, ids_ref[g], gid)
        bias_g = jnp.where(jnp.abs(gid - q_block) > width, 0.0, MASKED)
        rows = pl.ds(pl.multiple_of(lb * BLOCK, BLOCK), BLOCK)
        wrows = pl.ds(pl.multiple_of(lb * BLOCK, BLOCK), window)
        for h in range(hd):
            q = q_ref[h, rows]
            sw = lax.dot_general(q, win_ref[h, wrows], nt, preferred_element_type=jnp.float32)
            sg = lax.dot_general(q, glob_ref[h], nt, preferred_element_type=jnp.float32)
            sw = sw * EXP2_SCALE + bias_w
            sg = sg * EXP2_SCALE + bias_g
            top = jnp.maximum(
                jnp.max(sw, axis=1, keepdims=True), jnp.max(sg, axis=1, keepdims=True)
            )
            pw = jnp.exp2(sw - top)
            pg = jnp.exp2(sg - top)
            total = jnp.sum(pw, axis=1, keepdims=True) + jnp.sum(pg, axis=1, keepdims=True)
            acc = jnp.dot(
                pw.astype(jnp.bfloat16), win_ref[hd + h, wrows], preferred_element_type=jnp.float32
            ) + jnp.dot(
                pg.astype(jnp.bfloat16), glob_ref[hd + h], preferred_element_type=jnp.float32
            )
            out_ref[rows, h * HD:(h + 1) * HD] = (acc / total).astype(jnp.bfloat16)


def attend(nb, nu, band, global_ids, q, win, glob):
    hd, ctx, _ = q.shape
    smem = pl.BlockSpec(memory_space=pltpu.SMEM)
    vmem = pl.BlockSpec(memory_space=pltpu.VMEM)
    return pl.pallas_call(
        functools.partial(attend_kernel, nb, nu),
        out_shape=jax.ShapeDtypeStruct((ctx, hd * HD), jnp.bfloat16),
        in_specs=[smem, smem, vmem, vmem, vmem],
        out_specs=vmem,
        compiler_params=pltpu.CompilerParams(vmem_limit_bytes=VMEM_LIMIT),
    )(band, global_ids, q, win, glob)


def body(nb, nu, tokens, w_qkv, w_out, band, global_ids):
    q, win, glob = gather(nb, nu, global_ids, tokens, w_qkv)
    attended = attend(nb, nu, band, global_ids, q, win, glob)
    returned = lax.all_to_all(attended, "uly", split_axis=0, concat_axis=1, tiled=True)
    result = jnp.dot(returned, w_out, preferred_element_type=jnp.float32)
    return result.astype(jnp.bfloat16)


def solution(mesh):
    return jax.shard_map(
        functools.partial(body, mesh.shape["blk"], mesh.shape["uly"]),
        mesh=mesh,
        in_specs=(P(("blk", "uly"), None), P(), P(), P("blk"), P()),
        out_specs=P(("blk", "uly"), None),
        check_vma=False,
    )
```

```python
import functools
import math

import jax
import jax.numpy as jnp
from jax import lax
from jax.experimental import pallas as pl
from jax.experimental.pallas import tpu as pltpu
from jax.sharding import PartitionSpec as P

H = 8
HD = 128
BLOCK = 128
NGLOBAL = 4
REACH = 2
SLOTS = 2 * REACH + 1
VMEM_LIMIT = 56 * 1024 * 1024
EXP2_SCALE = math.log2(math.e) / HD**0.5
MASKED = -1e30


def gather_kernel(
    nb, nu, ids_ref, tok_ref, w_ref, q_ref, win_ref, glob_ref,
    qkv_ref, own_ref, pre_ref, suf_ref, up_ref, down_ref,
    a2a_s, a2a_r, x_s, x_r, c_s, c_r, f_s, f_r, z_s, z_r,
    up_s, up_r, dn_s, dn_r, gx_s, gx_r, gc_s, gc_r, gf_s, gf_r,
):
    tok = tok_ref.shape[0]
    hd = H // nu
    ctx = tok * nu
    bd = ctx // BLOCK
    nz = nb // 4
    half = NGLOBAL // 2
    nj = 2 * hd
    b = lax.axis_index("blk")
    u = lax.axis_index("uly")
    r = b % 4
    z = b // 4
    low = r < 2
    inner = (r == 1) | (r == 2)
    has_up = z < nz - 1
    has_dn = z > 0
    px = jnp.where(low, b + 2, b - 2)
    pc = jnp.where(r % 2 == 0, b + 1, b - 1)

    barrier = pltpu.get_barrier_semaphore()

    def greet(blk, uly):
        pl.semaphore_signal(
            barrier, inc=1, device_id=(blk, uly), device_id_type=pl.DeviceIdType.MESH
        )

    for d in range(1, nu):
        greet(b, (u + d) % nu)
    greet(px, u)
    greet(pc, u)
    pl.when(has_up)(lambda: greet(b + 4, u))
    pl.when(has_dn)(lambda: greet(b - 4, u))
    pl.semaphore_wait(
        barrier, nu + 1 + jnp.where(has_up, 1, 0) + jnp.where(has_dn, 1, 0)
    )

    def rdma(src, dst, s, rr, blk, uly):
        return pltpu.make_async_remote_copy(
            src_ref=src, dst_ref=dst, send_sem=s, recv_sem=rr,
            device_id=(blk, uly), device_id_type=pl.DeviceIdType.MESH,
        )

    def slot(j, s):
        return win_ref.at[j, pl.ds(pl.multiple_of(s * ctx, ctx), ctx)]

    def clear(s):
        win_ref[:, pl.ds(s * ctx, ctx), :] = jnp.zeros((nj, ctx, HD), jnp.bfloat16)

    pl.when(b < 2)(lambda: clear(0))
    pl.when(b < 1)(lambda: clear(1))
    pl.when(b > nb - 2)(lambda: clear(3))
    pl.when(b > nb - 3)(lambda: clear(4))

    def a2a(d, j, part, h):
        to = (u + d) % nu
        rows = pl.ds(pl.multiple_of(u * tok, tok), tok)
        if part == 0:
            dst = q_ref.at[h, rows]
        else:
            dst = win_ref.at[
                (part - 1) * hd + h, pl.ds(pl.multiple_of(2 * ctx + u * tok, tok), tok)
            ]
        return rdma(
            qkv_ref.at[part * H + to * hd + h], dst,
            a2a_s.at[d - 1, j], a2a_r.at[d - 1, j], b, to,
        )

    def chunks(part):
        return [(j, j - {1: 0, 2: hd, 0: 2 * hd}[part])
                for j in range({1: 0, 2: hd, 0: 2 * hd}[part], {1: hd, 2: 2 * hd, 0: 3 * hd}[part])]

    for part in (1, 2, 0):
        for p in range(H // 2):
            col = part * H * HD + p * 2 * HD
            res = jnp.dot(
                tok_ref[...], w_ref[:, col:col + 2 * HD], preferred_element_type=jnp.float32
            ).astype(jnp.bfloat16)
            qkv_ref[part * H + 2 * p] = res[:, :HD]
            qkv_ref[part * H + 2 * p + 1] = res[:, HD:]
        for j, h in chunks(part):
            for d in range(1, nu):
                a2a(d, j, part, h).start()
        for j, h in chunks(part):
            mine = qkv_ref[part * H + u * hd + h]
            if part == 0:
                q_ref[h, pl.ds(pl.multiple_of(u * tok, tok), tok)] = mine
            else:
                win_ref[j, pl.ds(pl.multiple_of(2 * ctx + u * tok, tok), tok)] = mine

    s_x = jnp.where(low, 0, 4)
    s_c = jnp.where(r % 2 == 0, 1, 3)
    in_x = 4 - s_x
    f_src = jnp.where((r == 0) | (r == 2), 4, 0)
    f_dst = jnp.where((r == 0) | (r == 2), 3, 1)

    def x_copy(j):
        return rdma(slot(j, 2), slot(j, s_x), x_s.at[j], x_r.at[j], px, u)

    def c_copy(j):
        return rdma(slot(j, 2), slot(j, s_c), c_s.at[j], c_r.at[j], pc, u)

    def f_copy(j):
        return rdma(slot(j, f_src), slot(j, f_dst), f_s.at[j], f_r.at[j], pc, u)

    z_to = jnp.where(low, b + 4, b - 4)
    z_sends = (low & has_up) | (~low & has_dn)
    z_gets = (low & has_dn) | (~low & has_up)
    f_sends = (r == 0) | (r == 3) | z_gets
    f_gets = inner | z_gets

    def z_copy(j):
        return rdma(slot(j, in_x), slot(j, s_x), z_s.at[j], z_r.at[j], z_to, u)

    def stage_a(j):
        part = 1 + j // hd
        for d in range(1, nu):
            a2a(d, j, part, j % hd).wait_recv()
        x_copy(j).start()
        c_copy(j).start()

    def stage_b(j):
        x_copy(j).wait_recv()
        pl.when((r == 0) | (r == 3))(lambda: f_copy(j).start())
        pl.when(z_sends)(lambda: z_copy(j).start())

    def stage_c(j):
        @pl.when(z_gets)
        def _():
            z_copy(j).wait_recv()
            pl.when(inner)(lambda: f_copy(j).start())
        c_copy(j).wait_recv()

        @pl.when(inner)
        def _():
            f_copy(j).wait_recv()
            first = jnp.where(r == 1, 1, 0)
            for g in range(half):
                gid = jnp.where(r == 1, ids_ref[g], ids_ref[half + g]) - 4 * z * bd

                def add(i, acc):
                    blk = win_ref[j, pl.ds(pl.multiple_of((first * bd + i) * BLOCK, BLOCK), BLOCK)]
                    take = jnp.where(gid == i, 1.0, 0.0).astype(jnp.float32)
                    return acc + blk.astype(jnp.float32) * take

                acc = lax.fori_loop(0, 4 * bd, add, jnp.zeros((BLOCK, HD), jnp.float32))
                own_ref[j, g * BLOCK:(g + 1) * BLOCK] = acc.astype(jnp.bfloat16)

    def up_copy(j):
        return rdma(up_ref.at[j], pre_ref.at[j], up_s.at[j], up_r.at[j], b + 4, u)

    def dn_copy(j):
        return rdma(down_ref.at[j], suf_ref.at[j], dn_s.at[j], dn_r.at[j], b - 4, u)

    def wait_in(kind, other, sem_s, sem_r, j):
        rdma(kind.at[j], kind.at[j], sem_s.at[j], sem_r.at[j], other, u).wait_recv()

    def stage_up(j):
        @pl.when(inner)
        def _():
            @pl.when(has_dn)
            def _():
                wait_in(pre_ref, b - 4, up_s, up_r, j)

            @pl.when(~has_dn)
            def _():
                pre_ref[j] = jnp.zeros((half * BLOCK, HD), jnp.bfloat16)

            @pl.when(has_up)
            def _():
                up_ref[j] = pre_ref[j] + own_ref[j]
                up_copy(j).start()

    a_half = pl.ds(0, half * BLOCK)
    b_half = pl.ds(half * BLOCK, half * BLOCK)
    mine_half = pl.ds(pl.multiple_of(jnp.where(r == 1, 0, half * BLOCK), BLOCK), half * BLOCK)
    fwd_half = pl.ds(pl.multiple_of(jnp.where(r == 0, half * BLOCK, 0), BLOCK), half * BLOCK)

    def gx_copy(j):
        return rdma(glob_ref.at[j, mine_half], glob_ref.at[j, mine_half],
                    gx_s.at[j], gx_r.at[j], px, u)

    def gc_copy(j):
        return rdma(glob_ref.at[j, mine_half], glob_ref.at[j, mine_half],
                    gc_s.at[j], gc_r.at[j], pc, u)

    def gf_copy(j):
        return rdma(glob_ref.at[j, fwd_half], glob_ref.at[j, fwd_half],
                    gf_s.at[j], gf_r.at[j], pc, u)

    def stage_down(j):
        @pl.when(inner)
        def _():
            @pl.when(has_up)
            def _():
                wait_in(suf_ref, b + 4, dn_s, dn_r, j)

            @pl.when(~has_up)
            def _():
                suf_ref[j] = jnp.zeros((half * BLOCK, HD), jnp.bfloat16)

            down_ref[j] = suf_ref[j] + own_ref[j]

            @pl.when(has_dn)
            def _():
                dn_copy(j).start()

    def stage_spread(j):
        @pl.when(inner)
        def _():
            glob_ref[j, mine_half] = down_ref[j] + pre_ref[j]
            gx_copy(j).start()
            gc_copy(j).start()

    def stage_out(j):
        @pl.when(~inner)
        def _():
            gx_copy(j).wait_recv()
            gf_copy(j).start()

    def sweep(j, stage):
        pl.when((j >= 0) & (j < nj))(lambda: stage(j))

    stages = [(0, stage_a), (1, stage_b), (2, stage_c), (2 + nz, stage_spread), (3 + nz, stage_out)]
    for t in range(nj + 3 + nz):
        for lag, stage in stages[:3]:
            if 0 <= t - lag < nj:
                stage(t - lag)
        if t >= 2:
            sweep(t - 2 - z, stage_up)
            sweep(t - 2 - (nz - 1 - z), stage_down)
        for lag, stage in stages[3:]:
            if 0 <= t - lag < nj:
                stage(t - lag)

    for part in (1, 2, 0):
        for j, h in chunks(part):
            for d in range(1, nu):
                a2a(d, j, part, h).wait_send()
                if part == 0:
                    a2a(d, j, part, h).wait_recv()
    for j in range(nj):
        x_copy(j).wait_send()
        c_copy(j).wait_send()
        pl.when(f_sends)(lambda: f_copy(j).wait_send())
        pl.when(z_sends)(lambda: z_copy(j).wait_send())
        pl.when(f_gets & ~inner)(lambda: f_copy(j).wait_recv())

        @pl.when(inner)
        def _():
            pl.when(has_up)(lambda: up_copy(j).wait_send())
            pl.when(has_dn)(lambda: dn_copy(j).wait_send())
            gx_copy(j).wait_send()
            gc_copy(j).wait_send()
            gf_copy(j).wait_recv()

        @pl.when(~inner)
        def _():
            gc_copy(j).wait_recv()
            gf_copy(j).wait_send()


def gather(nb, nu, global_ids, tokens, w_qkv):
    tok = tokens.shape[0]
    hd = H // nu
    ctx = tok * nu
    nj = 2 * hd
    part = pltpu.VMEM((nj, NGLOBAL // 2 * BLOCK, HD), jnp.bfloat16)
    dma = pltpu.SemaphoreType.DMA
    vmem = pl.BlockSpec(memory_space=pltpu.VMEM)
    return pl.pallas_call(
        functools.partial(gather_kernel, nb, nu),
        out_shape=[
            jax.ShapeDtypeStruct((hd, ctx, HD), jnp.bfloat16),
            jax.ShapeDtypeStruct((nj, SLOTS * ctx, HD), jnp.bfloat16),
            jax.ShapeDtypeStruct((nj, NGLOBAL * BLOCK, HD), jnp.bfloat16),
        ],
        in_specs=[pl.BlockSpec(memory_space=pltpu.SMEM), vmem, vmem],
        out_specs=[vmem, vmem, vmem],
        scratch_shapes=[
            pltpu.VMEM((3 * H, tok, HD), jnp.bfloat16), part, part, part, part, part,
            dma((nu - 1, 3 * hd)), dma((nu - 1, 3 * hd)),
        ] + [dma((nj,))] * 18,
        compiler_params=pltpu.CompilerParams(
            collective_id=0, has_side_effects=True, vmem_limit_bytes=VMEM_LIMIT
        ),
    )(global_ids, tokens, w_qkv)


def attend_kernel(nb, nu, band_ref, ids_ref, q_ref, win_ref, glob_ref, out_ref):
    hd = H // nu
    ctx = q_ref.shape[1]
    bd = ctx // BLOCK
    reach = REACH * bd
    window = (2 * reach + 1) * BLOCK
    b = lax.axis_index("blk")
    nt = (((1,), (1,)), ((), ()))

    @pl.loop(0, bd)
    def _(lb):
        q_block = b * bd + lb
        width = band_ref[lb]
        key = q_block - reach + lax.broadcasted_iota(jnp.int32, (1, window), 1) // BLOCK
        seen = (jnp.abs(key - q_block) <= width) & (key >= 0) & (key < nb * bd)
        bias_w = jnp.where(seen, 0.0, MASKED)
        lane = lax.broadcasted_iota(jnp.int32, (1, NGLOBAL * BLOCK), 1) // BLOCK
        gid = jnp.zeros_like(lane)
        for g in range(NGLOBAL):
            gid = jnp.where(lane == g, ids_ref[g], gid)
        bias_g = jnp.where(jnp.abs(gid - q_block) > width, 0.0, MASKED)
        rows = pl.ds(pl.multiple_of(lb * BLOCK, BLOCK), BLOCK)
        wrows = pl.ds(pl.multiple_of(lb * BLOCK, BLOCK), window)
        for h in range(hd):
            q = q_ref[h, rows]
            sw = lax.dot_general(q, win_ref[h, wrows], nt, preferred_element_type=jnp.float32)
            sg = lax.dot_general(q, glob_ref[h], nt, preferred_element_type=jnp.float32)
            sw = sw * EXP2_SCALE + bias_w
            sg = sg * EXP2_SCALE + bias_g
            top = jnp.maximum(
                jnp.max(sw, axis=1, keepdims=True), jnp.max(sg, axis=1, keepdims=True)
            )
            pw = jnp.exp2(sw - top)
            pg = jnp.exp2(sg - top)
            total = jnp.sum(pw, axis=1, keepdims=True) + jnp.sum(pg, axis=1, keepdims=True)
            acc = jnp.dot(
                pw.astype(jnp.bfloat16), win_ref[hd + h, wrows], preferred_element_type=jnp.float32
            ) + jnp.dot(
                pg.astype(jnp.bfloat16), glob_ref[hd + h], preferred_element_type=jnp.float32
            )
            out_ref[rows, h * HD:(h + 1) * HD] = (acc / total).astype(jnp.bfloat16)


def attend(nb, nu, band, global_ids, q, win, glob):
    hd, ctx, _ = q.shape
    smem = pl.BlockSpec(memory_space=pltpu.SMEM)
    vmem = pl.BlockSpec(memory_space=pltpu.VMEM)
    return pl.pallas_call(
        functools.partial(attend_kernel, nb, nu),
        out_shape=jax.ShapeDtypeStruct((ctx, hd * HD), jnp.bfloat16),
        in_specs=[smem, smem, vmem, vmem, vmem],
        out_specs=vmem,
        compiler_params=pltpu.CompilerParams(vmem_limit_bytes=VMEM_LIMIT),
    )(band, global_ids, q, win, glob)


def body(nb, nu, tokens, w_qkv, w_out, band, global_ids):
    q, win, glob = gather(nb, nu, global_ids, tokens, w_qkv)
    attended = attend(nb, nu, band, global_ids, q, win, glob)
    returned = lax.all_to_all(attended, "uly", split_axis=0, concat_axis=1, tiled=True)
    result = jnp.dot(returned, w_out, preferred_element_type=jnp.float32)
    return result.astype(jnp.bfloat16)


def solution(mesh):
    return jax.shard_map(
        functools.partial(body, mesh.shape["blk"], mesh.shape["uly"]),
        mesh=mesh,
        in_specs=(P(("blk", "uly"), None), P(), P(), P("blk"), P()),
        out_specs=P(("blk", "uly"), None),
        check_vma=False,
    )
```

```python
import functools
import math

import jax
import jax.numpy as jnp
from jax import lax
from jax.experimental import pallas as pl
from jax.experimental.pallas import tpu as pltpu
from jax.sharding import PartitionSpec as P

H = 8
HD = 128
BLOCK = 128
NGLOBAL = 4
REACH = 2
SLOTS = 2 * REACH + 1
VMEM_LIMIT = 56 * 1024 * 1024
EXP2_SCALE = math.log2(math.e) / HD**0.5
MASKED = -1e30


def layer_kernel(
    nb, nu, band_ref, ids_ref, tok_ref, w_ref, out_ref,
    q_ref, win_ref, glob_ref, far_ref, wbuf_ref, acc_ref, top_ref, sum_ref, att_ref,
    own_ref, pre_ref, suf_ref, up_ref, down_ref,
    w_sem, tok_s, tok_r, back_s, back_r, x_s, x_r, c_s, c_r, f_s, f_r, z_s, z_r,
    up_s, up_r, dn_s, dn_r, gx_s, gx_r, gc_s, gc_r, gf_s, gf_r,
):
    tok = tok_ref.shape[0]
    hd = H // nu
    ctx = tok * nu
    bd = ctx // BLOCK
    nz = nb // 4
    half = NGLOBAL // 2
    nj = 2 * hd
    hc = min(2, hd)
    ng = nj // hc
    tb = tok // BLOCK
    b = lax.axis_index("blk")
    u = lax.axis_index("uly")
    r = b % 4
    z = b // 4
    low = r < 2
    inner = (r == 1) | (r == 2)
    has_up = z < nz - 1
    has_dn = z > 0
    px = jnp.where(low, b + 2, b - 2)
    pc = jnp.where(r % 2 == 0, b + 1, b - 1)

    def w_load(part):
        cols = pl.ds(pl.multiple_of(part * H * HD + u * hd * HD, HD), hd * HD)
        return pltpu.make_async_copy(w_ref.at[:, cols], wbuf_ref.at[part], w_sem.at[part])

    for part in (1, 2, 0):
        w_load(part).start()

    barrier = pltpu.get_barrier_semaphore()

    def greet(blk, uly):
        pl.semaphore_signal(
            barrier, inc=1, device_id=(blk, uly), device_id_type=pl.DeviceIdType.MESH
        )

    for d in range(1, nu):
        greet(b, (u + d) % nu)
    greet(px, u)
    greet(pc, u)
    pl.when(has_up)(lambda: greet(b + 4, u))
    pl.when(has_dn)(lambda: greet(b - 4, u))
    pl.semaphore_wait(
        barrier, nu + 1 + jnp.where(has_up, 1, 0) + jnp.where(has_dn, 1, 0)
    )

    def rdma(src, dst, s, rr, blk, uly):
        return pltpu.make_async_remote_copy(
            src_ref=src, dst_ref=dst, send_sem=s, recv_sem=rr,
            device_id=(blk, uly), device_id_type=pl.DeviceIdType.MESH,
        )

    def rows_of(d):
        return ((u + d) % nu) * tok

    def slot(c, s):
        d, g = c // ng, c % ng
        j0 = g % 2 * hd + g // 2 * hc
        return win_ref.at[pl.ds(j0, hc), pl.ds(pl.multiple_of(s * ctx + rows_of(d), tok), tok)]

    def heads_of(g):
        return pl.ds(g % 2 * hd + g // 2 * hc, hc)

    def tok_copy(d):
        return rdma(tok_ref, far_ref.at[d - 1], tok_s.at[d - 1], tok_r.at[d - 1], b, (u + d) % nu)

    for d in range(1, nu):
        tok_copy(d).start()

    def clear(s):
        win_ref[:, pl.ds(s * ctx, ctx), :] = jnp.zeros((nj, ctx, HD), jnp.bfloat16)

    pl.when(b < 2)(lambda: clear(0))
    pl.when(b < 1)(lambda: clear(1))
    pl.when(b > nb - 2)(lambda: clear(3))
    pl.when(b > nb - 3)(lambda: clear(4))

    def project(d, part):
        src = (nu - d) % nu
        toks = tok_ref[...] if src == 0 else far_ref[src - 1]
        res = jnp.dot(toks, wbuf_ref[part], preferred_element_type=jnp.float32)
        res = res.astype(jnp.bfloat16)
        for h in range(hd):
            one = res[:, h * HD:(h + 1) * HD]
            if part == 0:
                q_ref[h, pl.ds(pl.multiple_of(rows_of(d), tok), tok)] = one
            else:
                at = pl.ds(pl.multiple_of(2 * ctx + rows_of(d), tok), tok)
                win_ref[(part - 1) * hd + h, at] = one

    s_x = jnp.where(low, 0, 4)
    s_c = jnp.where(r % 2 == 0, 1, 3)
    in_x = 4 - s_x
    f_src = jnp.where((r == 0) | (r == 2), 4, 0)
    f_dst = jnp.where((r == 0) | (r == 2), 3, 1)

    def x_copy(j):
        return rdma(slot(j, 2), slot(j, s_x), x_s.at[j], x_r.at[j], px, u)

    def c_copy(j):
        return rdma(slot(j, 2), slot(j, s_c), c_s.at[j], c_r.at[j], pc, u)

    def f_copy(j):
        return rdma(slot(j, f_src), slot(j, f_dst), f_s.at[j], f_r.at[j], pc, u)

    z_to = jnp.where(low, b + 4, b - 4)
    z_sends = (low & has_up) | (~low & has_dn)
    z_gets = (low & has_dn) | (~low & has_up)
    f_sends = (r == 0) | (r == 3) | z_gets
    f_gets = inner | z_gets

    def z_copy(j):
        return rdma(slot(j, in_x), slot(j, s_x), z_s.at[j], z_r.at[j], z_to, u)

    def stage_a(c):
        d, g = c // ng, c % ng
        if g == 0 and d > 0:
            tok_copy(nu - d).wait_recv()
        if g < 2:
            if d == 0:
                w_load(1 + g).wait()
            project(d, 1 + g)
        x_copy(c).start()
        c_copy(c).start()
        if g == ng - 1:
            if d == 0:
                w_load(0).wait()
            project(d, 0)

    def stage_b(j):
        x_copy(j).wait_recv()
        pl.when((r == 0) | (r == 3))(lambda: f_copy(j).start())
        pl.when(z_sends)(lambda: z_copy(j).start())

    def stage_c(c):
        @pl.when(z_gets)
        def _():
            z_copy(c).wait_recv()
            pl.when(inner)(lambda: f_copy(c).start())
        c_copy(c).wait_recv()
        pl.when(inner)(lambda: f_copy(c).wait_recv())

    def stage_f(c):
        pl.when(f_gets & ~inner)(lambda: f_copy(c).wait_recv())

    def pick(g0):
        @pl.when(inner)
        def _():
            first = jnp.where(r == 1, 1, 0)
            for g in range(half):
                gid = jnp.where(r == 1, ids_ref[g], ids_ref[half + g]) - 4 * z * bd

                def add(i, acc):
                    at = pl.ds(pl.multiple_of((first * bd + i) * BLOCK, BLOCK), BLOCK)
                    take = jnp.where(gid == i, 1.0, 0.0).astype(jnp.float32)
                    return acc + win_ref[heads_of(g0), at].astype(jnp.float32) * take

                acc = lax.fori_loop(0, 4 * bd, add, jnp.zeros((hc, BLOCK, HD), jnp.float32))
                own_ref[g0, :, g * BLOCK:(g + 1) * BLOCK] = acc.astype(jnp.bfloat16)

    def up_copy(j):
        return rdma(up_ref.at[j], pre_ref.at[j], up_s.at[j], up_r.at[j], b + 4, u)

    def dn_copy(j):
        return rdma(down_ref.at[j], suf_ref.at[j], dn_s.at[j], dn_r.at[j], b - 4, u)

    def wait_in(kind, other, sem_s, sem_r, j):
        rdma(kind.at[j], kind.at[j], sem_s.at[j], sem_r.at[j], other, u).wait_recv()

    def stage_up(j):
        @pl.when(inner)
        def _():
            @pl.when(has_dn)
            def _():
                wait_in(pre_ref, b - 4, up_s, up_r, j)

            @pl.when(~has_dn)
            def _():
                pre_ref[j] = jnp.zeros((hc, half * BLOCK, HD), jnp.bfloat16)

            @pl.when(has_up)
            def _():
                up_ref[j] = pre_ref[j] + own_ref[j]
                up_copy(j).start()

    mine_half = pl.ds(pl.multiple_of(jnp.where(r == 1, 0, half * BLOCK), BLOCK), half * BLOCK)
    fwd_half = pl.ds(pl.multiple_of(jnp.where(r == 0, half * BLOCK, 0), BLOCK), half * BLOCK)

    def gx_copy(j):
        return rdma(glob_ref.at[heads_of(j), mine_half], glob_ref.at[heads_of(j), mine_half],
                    gx_s.at[j], gx_r.at[j], px, u)

    def gc_copy(j):
        return rdma(glob_ref.at[heads_of(j), mine_half], glob_ref.at[heads_of(j), mine_half],
                    gc_s.at[j], gc_r.at[j], pc, u)

    def gf_copy(j):
        return rdma(glob_ref.at[heads_of(j), fwd_half], glob_ref.at[heads_of(j), fwd_half],
                    gf_s.at[j], gf_r.at[j], pc, u)

    def stage_down(j):
        @pl.when(inner)
        def _():
            @pl.when(has_up)
            def _():
                wait_in(suf_ref, b + 4, dn_s, dn_r, j)

            @pl.when(~has_up)
            def _():
                suf_ref[j] = jnp.zeros((hc, half * BLOCK, HD), jnp.bfloat16)

            down_ref[j] = suf_ref[j] + own_ref[j]

            @pl.when(has_dn)
            def _():
                dn_copy(j).start()

    def stage_spread(j):
        @pl.when(inner)
        def _():
            glob_ref[heads_of(j), mine_half] = down_ref[j] + pre_ref[j]
            gx_copy(j).start()
            gc_copy(j).start()

    def stage_out(j):
        @pl.when(~inner)
        def _():
            gx_copy(j).wait_recv()
            gf_copy(j).start()

    reach = REACH * bd
    window = (2 * reach + 1) * BLOCK
    nt = (((1,), (1,)), ((), ()))

    def attend_window(n):
        lb = n % bd
        q_block = b * bd + lb
        key = q_block - reach + lax.broadcasted_iota(jnp.int32, (1, window), 1) // BLOCK
        seen = (jnp.abs(key - q_block) <= band_ref[lb]) & (key >= 0) & (key < nb * bd)
        bias = jnp.where(seen, 0.0, MASKED)
        rows = pl.ds(lb * BLOCK, BLOCK)
        wrows = pl.ds(lb * BLOCK, window)
        for h in range(n // bd * hc, (n // bd + 1) * hc):
            sw = lax.dot_general(
                q_ref[h, rows], win_ref[h, wrows], nt, preferred_element_type=jnp.float32
            )
            sw = sw * EXP2_SCALE + bias
            top = jnp.max(sw, axis=1, keepdims=True)
            pw = jnp.exp2(sw - top)
            top_ref[h, rows] = top
            sum_ref[h, rows] = jnp.sum(pw, axis=1, keepdims=True)
            acc_ref[h, rows] = jnp.dot(
                pw.astype(jnp.bfloat16), win_ref[hd + h, wrows], preferred_element_type=jnp.float32
            )

    def back_copy(k, at_rows, to):
        return rdma(
            att_ref.at[k],
            out_ref.at[pl.ds(pl.multiple_of(at_rows, BLOCK), BLOCK),
                       pl.ds(pl.multiple_of(u * hd * HD, HD), hd * HD)],
            back_s.at[k], back_r.at[k], b, to,
        )

    def finish(k):
        d = k // tb + 1
        to = (u + d) % nu
        lb = to * tb + k % tb
        q_block = b * bd + lb
        lane = lax.broadcasted_iota(jnp.int32, (1, NGLOBAL * BLOCK), 1) // BLOCK
        gid = jnp.zeros_like(lane)
        for g in range(NGLOBAL):
            gid = jnp.where(lane == g, ids_ref[g], gid)
        bias = jnp.where(jnp.abs(gid - q_block) > band_ref[lb], 0.0, MASKED)
        rows = pl.ds(pl.multiple_of(lb * BLOCK, BLOCK), BLOCK)
        for h in range(hd):
            sg = lax.dot_general(
                q_ref[h, rows], glob_ref[h], nt, preferred_element_type=jnp.float32
            )
            sg = sg * EXP2_SCALE + bias
            top = jnp.maximum(top_ref[h, rows], jnp.max(sg, axis=1, keepdims=True))
            pg = jnp.exp2(sg - top)
            old = jnp.exp2(top_ref[h, rows] - top)
            total = sum_ref[h, rows] * old + jnp.sum(pg, axis=1, keepdims=True)
            acc = acc_ref[h, rows] * old + jnp.dot(
                pg.astype(jnp.bfloat16), glob_ref[hd + h], preferred_element_type=jnp.float32
            )
            one = (acc / total).astype(jnp.bfloat16)
            if d < nu:
                att_ref[k, :, h * HD:(h + 1) * HD] = one
            else:
                out_ref[k % tb * BLOCK:(k % tb + 1) * BLOCK,
                        pl.ds(pl.multiple_of((u * hd + h) * HD, HD), HD)] = one
        if d < nu:
            back_copy(k, k % tb * BLOCK, to).start()

    def sweep(j, stage):
        pl.when((j >= 0) & (j < ng))(lambda: stage(j))

    nc = nu * ng
    t0 = nc - ng + 4
    steps = range(t0 + 2, t0 + ng + nz + 1)
    units = hd // hc * bd
    for t in range(t0 + ng + nz + 1):
        for lag, stage in ((0, stage_a), (2, stage_b), (4, stage_c)):
            if 0 <= t - lag < nc:
                stage(t - lag)
        if 0 <= t - t0 < ng:
            pick(t - t0)
        if t >= t0:
            sweep(t - t0 - z, stage_up)
            sweep(t - t0 - (nz - 1 - z), stage_down)
        for lag, stage in ((t0 + nz, stage_spread), (t0 + nz + 1, stage_out)):
            if 0 <= t - lag < ng:
                stage(t - lag)
        if 0 <= t - 5 < nc:
            stage_f(t - 5)
        for n in range(units):
            if t == max(steps[n * len(steps) // units], t0 + 2 + n // bd * 2):
                attend_window(n)

    for j in range(ng):
        pl.when(inner)(lambda: gf_copy(j).wait_recv())
        pl.when(~inner)(lambda: gc_copy(j).wait_recv())
    for k in range(bd):
        finish(k)

    for d in range(1, nu):
        tok_copy(d).wait_send()
    for c in range(nc):
        x_copy(c).wait_send()
        c_copy(c).wait_send()
        pl.when(f_sends)(lambda: f_copy(c).wait_send())
        pl.when(z_sends)(lambda: z_copy(c).wait_send())
    for j in range(ng):
        @pl.when(inner)
        def _():
            pl.when(has_up)(lambda: up_copy(j).wait_send())
            pl.when(has_dn)(lambda: dn_copy(j).wait_send())
            gx_copy(j).wait_send()
            gc_copy(j).wait_send()

        pl.when(~inner)(lambda: gf_copy(j).wait_send())
    for k in range(bd - tb):
        back_copy(k, k % tb * BLOCK, (u + k // tb + 1) % nu).wait()


def layer(nb, nu, band, global_ids, tokens, w_qkv):
    tok, width = tokens.shape
    hd = H // nu
    ctx = tok * nu
    bd = ctx // BLOCK
    nj = 2 * hd
    hc = min(2, hd)
    ng = nj // hc
    back = bd - tok // BLOCK
    share = pltpu.VMEM((ng, hc, NGLOBAL // 2 * BLOCK, HD), jnp.bfloat16)
    dma = pltpu.SemaphoreType.DMA
    smem = pl.BlockSpec(memory_space=pltpu.SMEM)
    vmem = pl.BlockSpec(memory_space=pltpu.VMEM)
    return pl.pallas_call(
        functools.partial(layer_kernel, nb, nu),
        out_shape=jax.ShapeDtypeStruct((tok, H * HD), jnp.bfloat16),
        in_specs=[smem, smem, vmem, pl.BlockSpec(memory_space=pl.ANY)],
        out_specs=vmem,
        scratch_shapes=[
            pltpu.VMEM((hd, ctx, HD), jnp.bfloat16),
            pltpu.VMEM((nj, SLOTS * ctx, HD), jnp.bfloat16),
            pltpu.VMEM((nj, NGLOBAL * BLOCK, HD), jnp.bfloat16),
            pltpu.VMEM((nu - 1, tok, width), jnp.bfloat16),
            pltpu.VMEM((3, width, hd * HD), jnp.bfloat16),
            pltpu.VMEM((hd, ctx, HD), jnp.float32),
            pltpu.VMEM((hd, ctx, 1), jnp.float32),
            pltpu.VMEM((hd, ctx, 1), jnp.float32),
            pltpu.VMEM((back, BLOCK, hd * HD), jnp.bfloat16),
            share, share, share, share, share,
            dma((3,)), dma((nu - 1,)), dma((nu - 1,)), dma((back,)), dma((back,)),
        ] + [dma((nu * ng,))] * 8 + [dma((ng,))] * 10,
        compiler_params=pltpu.CompilerParams(
            collective_id=0, has_side_effects=True, vmem_limit_bytes=VMEM_LIMIT
        ),
    )(band, global_ids, tokens, w_qkv)


def body(nb, nu, tokens, w_qkv, w_out, band, global_ids):
    attended = layer(nb, nu, band, global_ids, tokens, w_qkv)
    result = jnp.dot(attended, w_out, preferred_element_type=jnp.float32)
    return result.astype(jnp.bfloat16)


def solution(mesh):
    return jax.shard_map(
        functools.partial(body, mesh.shape["blk"], mesh.shape["uly"]),
        mesh=mesh,
        in_specs=(P(("blk", "uly"), None), P(), P(), P("blk"), P()),
        out_specs=P(("blk", "uly"), None),
        check_vma=False,
    )
```
